32 devices in a mesh: head: 4 (over x, core), blk: 8 (over z, y).
Axes of the slice: x: 2, y: 2, z: 4, core: 2. Of those that a mesh axis runs over, the one named last changes fastest.
Arguments:
- queries: bfloat16 [8, 128, 6144], P('blk', 'head'), may hold values from -6 to 6
- keys: bfloat16 [8, 128, 6144], P('blk', 'head'), may hold values from -6 to 6
- values: bfloat16 [8, 128, 6144], P('blk', 'head'), may hold values from -6 to 6
- out_grad: bfloat16 [8, 128, 6144], P('blk', 'head'), may hold values from -96 to 96
- log_sum_exp: bfloat16 [48, 8, 128], P('head', 'blk'), may hold values from 7 to 9
- row_delta: bfloat16 [48, 8, 128], P('head', 'blk'), may hold values from -180 to 180
- assignment: int32 [8], replicated, may hold values from 0 to 7, as said below
- block_mask: int32 [16, 16], replicated, may hold values from 0 to 2, as said below
Outputs:
- query_grad: bfloat16 [8, 128, 6144], P('blk', 'head')
- key_grad: bfloat16 [8, 128, 6144], P('blk', 'head')
- value_grad: bfloat16 [8, 128, 6144], P('blk', 'head')
The draws below stay inside these ranges and needn't reach their ends.
Inputs may be any that keep to these rules, and one draw needn't show every extreme that they name: A permutation of the pair indices; the slot d holds the blocks assignment[d] and 15 - assignment[d]. `block_mask`: 2 on the diagonal; 1 where the key block comes earlier than the query block and the slots holding the two blocks lie at most 2 apart around the cyclic order of slots; 0 elsewhere.
All inputs are finite; a program needn't handle non-finite values.
Results may differ from the reference program's by a relative error of at most 0.008.
Values may be sent and summed in bfloat16 or wider, within the bound.
A program may use at most 64 MiB of HBM per device.

```python
import jax
import jax.numpy as jnp
from jax import lax

HEADS = 48
HD = 128
BS = 64
HW = 6144
CYCLE = 2
N_BLK = 8


def shared_ordering(key):
    return jax.random.permutation(key, N_BLK).astype(jnp.int32)


def draw_assignment(key, part):
    ordering = shared_ordering(key)
    return ordering


def draw_block_mask(key, part):
    ordering = shared_ordering(key)
    owners = jnp.zeros((N_BLK,), jnp.int32).at[ordering].set(jnp.arange(N_BLK, dtype=jnp.int32))
    blocks = jnp.arange(2 * N_BLK, dtype=jnp.int32)
    pair_of = jnp.minimum(blocks, 2 * N_BLK - 1 - blocks)
    device_of = owners[pair_of]
    distance = jnp.mod(device_of[None, :] - device_of[:, None], N_BLK)
    nearby = jnp.minimum(distance, N_BLK - distance) <= CYCLE
    earlier = (blocks[None, :] < blocks[:, None]) & nearby
    diagonal = blocks[:, None] == blocks[None, :]
    return jnp.where(diagonal, 2, jnp.where(earlier, 1, 0)).astype(jnp.int32)


def level_of(rng, shape, cuts, low, largest):
    level, own = 1.0, jax.random.fold_in(rng, 6)
    for dim, parts in cuts:
        heights = jnp.exp(jax.random.uniform(jax.random.fold_in(own, dim), (parts,), jnp.float32, low / len(cuts), largest / len(cuts)))
        level = level * jnp.repeat(heights, shape[dim] // parts).reshape([-1 if axis == dim else 1 for axis in range(len(shape))])
    return level


def normal_values(stream_key, dims, width, limit, shards=(), kind=jnp.bfloat16):
    level = level_of(stream_key, dims, shards, -0.22, 0.18) if shards else 1.0
    array = jax.random.normal(stream_key, dims, jnp.float32) * width * level
    return jnp.minimum(jnp.maximum(array, -limit), limit).astype(kind)


def setup_inputs(seed: int = 0) -> dict:
    key_list = jax.random.split(jax.random.key(seed), 9)
    queries = normal_values(key_list[0], (N_BLK, 2 * BS, HW), 1.0, 6.0, ((0, 8), (1, 4)))
    keys = normal_values(key_list[1], (N_BLK, 2 * BS, HW), 1.0, 6.0, ((0, 8), (1, 4)))
    values = normal_values(key_list[2], (N_BLK, 2 * BS, HW), 1.0, 6.0, ((0, 8), (1, 4)))
    out_grad = normal_values(key_list[3], (N_BLK, 2 * BS, HW), 16.0, 96.0, ((0, 8), (1, 4)))
    log_sum_exp = jnp.clip(7.0 + 2.0 * jax.random.uniform(key_list[4], (HEADS, N_BLK, 2 * BS), jnp.float32) ** level_of(key_list[4], (HEADS, N_BLK, 2 * BS), ((0, 4), (1, 8)), -0.2, 0.2), 7.0, 9.0).astype(jnp.bfloat16)
    row_delta = normal_values(key_list[5], (HEADS, N_BLK, 2 * BS), 30.0, 180.0, ((0, 4), (1, 8)))
    assignment = draw_assignment(jax.random.fold_in(key_list[8], 71), 0)
    block_mask = draw_block_mask(jax.random.fold_in(key_list[8], 71), 0)
    return {"queries": queries, "keys": keys, "values": values, "out_grad": out_grad, "log_sum_exp": log_sum_exp, "row_delta": row_delta, "assignment": assignment, "block_mask": block_mask}


def slot_blocks(assignment, device):
    pair_index = assignment[device]
    row_ids = jnp.arange(2 * BS, dtype=jnp.int32)
    blocks = jnp.where(row_ids < BS, pair_index, 2 * N_BLK - 1 - pair_index).astype(jnp.int32)
    return blocks, row_ids % BS


def pair_terms(query_rows, grad_rows, lse_rows, delta_rows, key_rows, value_rows, allowed):
    scaling = HD ** -0.5
    row_count = query_rows.shape[0]
    q_float = query_rows.astype(jnp.float32).reshape(row_count, HEADS, HD)
    g_float = grad_rows.astype(jnp.float32).reshape(row_count, HEADS, HD)
    k_float = key_rows.astype(jnp.float32).reshape(row_count, HEADS, HD)
    v_float = value_rows.astype(jnp.float32).reshape(row_count, HEADS, HD)
    scores = jnp.einsum('qhd,khd->hqk', q_float, k_float) * scaling
    probabilities = jnp.where(allowed[None], jnp.exp(scores - lse_rows.astype(jnp.float32)[:, :, None]), 0.0)
    prob_bf = probabilities.astype(jnp.bfloat16).astype(jnp.float32)
    dprobs = jnp.einsum('qhd,khd->hqk', g_float, v_float)
    dscores = (probabilities * (dprobs - delta_rows.astype(jnp.float32)[:, :, None])).astype(jnp.bfloat16).astype(jnp.float32)
    dv_part = jnp.einsum('hqk,qhd->khd', prob_bf, g_float).reshape(row_count, HW).astype(jnp.bfloat16)
    dk_part = (scaling * jnp.einsum('hqk,qhd->khd', dscores, q_float)).reshape(row_count, HW).astype(jnp.bfloat16)
    dq_part = (scaling * jnp.einsum('hqk,khd->qhd', dscores, k_float)).reshape(row_count, HW).astype(jnp.bfloat16)
    return dq_part, dk_part, dv_part


def reference(queries, keys, values, out_grad, log_sum_exp, row_delta, assignment, block_mask):
    def one_slot(totals, slot):
        dk_total, dv_total = totals
        q_blocks, q_offsets = slot_blocks(assignment, slot)
        query_rows = queries[slot]
        grad_rows = out_grad[slot]
        lse_rows = log_sum_exp[:, slot, :]
        delta_rows = row_delta[:, slot, :]
        dq_total = jnp.zeros((2 * BS, HW), jnp.float32)
        for offset in range(-CYCLE, CYCLE + 1):
            other = jnp.mod(slot + offset, N_BLK).astype(jnp.int32)
            k_blocks, k_offsets = slot_blocks(assignment, other)
            table = block_mask[q_blocks[:, None], k_blocks[None, :]]
            allowed = (table == 1) | ((table == 2) & (q_offsets[:, None] >= k_offsets[None, :]))
            dq_part, dk_part, dv_part = pair_terms(query_rows, grad_rows, lse_rows, delta_rows, keys[other], values[other], allowed)
            dq_total = dq_total + dq_part.astype(jnp.float32)
            dk_total = dk_total.at[other].add(dk_part.astype(jnp.float32))
            dv_total = dv_total.at[other].add(dv_part.astype(jnp.float32))
        return (dk_total, dv_total), dq_total.astype(jnp.bfloat16)

    start = (jnp.zeros((N_BLK, 2 * BS, HW), jnp.float32), jnp.zeros((N_BLK, 2 * BS, HW), jnp.float32))
    (dk_total, dv_total), query_grad = lax.scan(one_slot, start, jnp.arange(N_BLK, dtype=jnp.int32))
    return query_grad, dk_total.astype(jnp.bfloat16), dv_total.astype(jnp.bfloat16)
```

```python
import functools

import jax
import jax.numpy as jnp
from jax import lax
from jax.experimental import pallas as pl
from jax.experimental.pallas import tpu as pltpu
from jax.sharding import PartitionSpec as P

HD = 128
LOG2E = 1.4426950408889634
BIG = 1e30
CHUNKS = 4
LANE_PAD = 16


def kernel(
    n_head,
    n_blk,
    mults,
    q_ref, k_ref, v_ref, g_ref, ld_ref, assign_ref, mask_ref,
    dq_out, dk_out, dv_out,
    qgkv, rqg, rld, bias, dq_acc, dkv_acc, fin, dq_send, dq_recv,
    in_send, in_recv, ld_send, ld_recv, f_send, f_recv, b_send, b_recv, o_send, o_recv,
):
    rows = q_ref.shape[1]
    width = q_ref.shape[2] // n_head
    total_rows = rows * n_head
    half = total_rows // 2
    heads = width // HD
    hc = heads // CHUNKS
    cw = hc * HD
    scaling = HD ** -0.5
    n_rel = len(mults)
    hi = lax.axis_index("head")
    me = lax.axis_index("blk")
    sign = 1 - 2 * lax.rem(me, 2)
    slots = [lax.rem(me + m * sign + 2 * n_blk, n_blk) for m in mults]
    landing = [i if m % 2 else mults.index(-m) for i, m in enumerate(mults)]
    partners = [lax.rem(hi + r, n_head) for r in range(1, n_head)]
    outs = (dq_out, dk_out, dv_out)

    barrier = pltpu.get_barrier_semaphore()
    for p in partners:
        pl.semaphore_signal(barrier, inc=1, device_id={"head": p}, device_id_type=pl.DeviceIdType.MESH)
    for s in slots:
        pl.semaphore_signal(barrier, inc=1, device_id={"blk": s}, device_id_type=pl.DeviceIdType.MESH)
    pl.semaphore_wait(barrier, n_head - 1 + n_rel)

    def remote(src, dst, send, recv, where):
        return pltpu.make_async_remote_copy(
            src_ref=src, dst_ref=dst, send_sem=send, recv_sem=recv,
            device_id=where, device_id_type=pl.DeviceIdType.MESH,
        )

    def chunk(c):
        return pl.ds(pl.multiple_of(c * cw, HD), cw)

    my_rows = pl.ds(pl.multiple_of(hi * rows, rows), rows)
    my_cols = pl.ds(pl.multiple_of(hi * width, HD), width)

    def in_copy(array, ref, r, c):
        p = partners[r]
        return remote(
            ref.at[0, :, pl.ds(pl.multiple_of(p * width + c * cw, HD), cw)],
            qgkv.at[array, my_rows, chunk(c)],
            in_send.at[array, r, c], in_recv.at[array, r, c], {"head": p},
        )

    def ld_copy(i):
        return remote(ld_ref, rld.at[landing[i]], ld_send.at[i], ld_recv.at[landing[i]], {"blk": slots[i]})

    def ld_wait(i):
        remote(ld_ref, rld.at[i], ld_send.at[i], ld_recv.at[i], {"blk": slots[i]}).wait_recv()

    def f_copy(i, c, a):
        if mults[i] == -1:
            return remote(rqg.at[1, a, :, chunk(c)], rqg.at[3, a, :, chunk(c)],
                          f_send.at[i, a, c], f_recv.at[i, a, c], {"blk": slots[0]})
        j = landing[i]
        return remote(qgkv.at[a, :, chunk(c)], rqg.at[j, a, :, chunk(c)],
                      f_send.at[i, a, c], f_recv.at[j, a, c], {"blk": slots[i]})

    def f_wait(i, c):
        for a in range(2):
            remote(qgkv.at[a, :, chunk(c)], rqg.at[i, a, :, chunk(c)],
                   f_send.at[i, a, c], f_recv.at[i, a, c], {"blk": slots[i]}).wait_recv()

    def b_copy(i, c):
        if mults[i] == -1:
            j, where = 3, slots[0]
        else:
            j, where = landing[i], slots[i]
        return remote(dq_send.at[i, :, chunk(c)], dq_recv.at[j, :, chunk(c)],
                      b_send.at[i, c], b_recv.at[j, c], {"blk": where})

    def b_wait(i, c):
        remote(dq_send.at[i, :, chunk(c)], dq_recv.at[i, :, chunk(c)],
               b_send.at[i, c], b_recv.at[i, c], {"blk": slots[i]}).wait_recv()

    def o_copy(array, r, c):
        p = partners[r]
        return remote(
            fin.at[array, pl.ds(pl.multiple_of(p * rows, rows), rows), chunk(c)],
            outs[array].at[0, :, pl.ds(pl.multiple_of(hi * width + c * cw, HD), cw)],
            o_send.at[array, r, c], o_recv.at[array, r, c], {"head": p},
        )

    for arrays in ((0, 1), (2, 3)):
        for c in range(CHUNKS):
            for array in arrays:
                for r in range(n_head - 1):
                    in_copy(array, (q_ref, g_ref, k_ref, v_ref)[array], r, c).start()
    for i in range(n_rel):
        ld_copy(i).start()
    for array, ref in enumerate((q_ref, g_ref, k_ref, v_ref)):
        qgkv[array, my_rows, :] = ref[0, :, my_cols]

    key_ids = lax.broadcasted_iota(jnp.int32, (total_rows, total_rows), 0)
    query_ids = lax.broadcasted_iota(jnp.int32, (total_rows, total_rows), 1)
    key_low, query_low = key_ids < half, query_ids < half
    later = lax.rem(query_ids, half) >= lax.rem(key_ids, half)
    k_first = assign_ref[me]
    k_second = 2 * n_blk - 1 - k_first
    for i, s in enumerate([me] + slots):
        q_first = assign_ref[s]
        q_second = 2 * n_blk - 1 - q_first
        table = jnp.where(
            query_low,
            jnp.where(key_low, mask_ref[q_first, k_first], mask_ref[q_first, k_second]),
            jnp.where(key_low, mask_ref[q_second, k_first], mask_ref[q_second, k_second]),
        )
        allowed = (table == 1) | ((table == 2) & later)
        bias[i] = jnp.where(allowed, 0.0, -BIG)

    @pl.loop(0, CHUNKS)
    def _(c):
        for array in range(2):
            for r in range(n_head - 1):
                in_copy(array, (q_ref, g_ref)[array], r, c).wait_recv()
        for i, m in enumerate(mults):
            if m != -1:
                for a in range(2):
                    f_copy(i, c, a).start()

    for i in range(n_rel):
        ld_wait(i)

    def pair(which, c, q_of, g_of, ld_of, first, emit):
        for h in range(hc):
            head = c * hc + h
            cols = pl.ds(pl.multiple_of(head * HD, HD), HD)
            q, g, k, v = q_of(cols), g_of(cols), qgkv[2, :, cols], qgkv[3, :, cols]
            lse = ld_of[pl.ds(head, 1), :] * LOG2E
            delta = ld_of[pl.ds(LANE_PAD + head, 1), :]
            contract = (((1,), (1,)), ((), ()))
            s = lax.dot_general(k, q, contract, preferred_element_type=jnp.float32)
            p = jnp.exp2(s * (scaling * LOG2E) - lse + bias[which])
            dp = lax.dot_general(v, g, contract, preferred_element_type=jnp.float32)
            ds = (p * (dp - delta)).astype(jnp.bfloat16)
            dv = jnp.dot(p.astype(jnp.bfloat16), g, preferred_element_type=jnp.float32)
            dk = jnp.dot(ds, q, preferred_element_type=jnp.float32)
            dq = lax.dot_general(ds, k, (((0,), (0,)), ((), ())), preferred_element_type=jnp.float32)
            if first:
                dkv_acc[0, :, cols] = dk
                dkv_acc[1, :, cols] = dv
            else:
                dkv_acc[0, :, cols] += dk
                dkv_acc[1, :, cols] += dv
            emit(cols, dq * scaling)

    def own(c):
        def emit(cols, dq):
            dq_acc[:, cols] = dq
        pair(0, c, lambda x: qgkv[0, :, x], lambda x: qgkv[1, :, x], ld_ref, True, emit)

    def other(i, c):
        def emit(cols, dq):
            dq_send[i, :, cols] = dq.astype(jnp.bfloat16)
        pair(i + 1, c, lambda x: rqg[i, 0, :, x], lambda x: rqg[i, 1, :, x], rld.at[i], False, emit)

    def finish(array, c, value):
        fin[array, :, chunk(c)] = value.astype(jnp.bfloat16)
        for r in range(n_head - 1):
            o_copy(array, r, c).start()
        outs[array][0, :, pl.ds(pl.multiple_of(hi * width + c * cw, HD), cw)] = fin[array, my_rows, chunk(c)]

    direct = [i for i, m in enumerate(mults) if m != -1]

    @pl.loop(0, CHUNKS + 3)
    def _(step):
        @pl.when(step < CHUNKS)
        def _():
            c = step
            for array in (2, 3):
                for r in range(n_head - 1):
                    in_copy(array, (q_ref, g_ref, k_ref, v_ref)[array], r, c).wait_recv()
            own(c)
            f_wait(1, c)
            for a in range(2):
                f_copy(3, c, a).start()
            for i in direct:
                if i != 1:
                    f_wait(i, c)
                    other(i, c)
                    b_copy(i, c).start()
            other(1, c)

        @pl.when((step >= 1) & (step < CHUNKS + 1))
        def _():
            c = step - 1
            f_wait(3, c)
            other(3, c)
            b_copy(3, c).start()
            finish(1, c, dkv_acc[0, :, chunk(c)] * scaling)
            finish(2, c, dkv_acc[1, :, chunk(c)])

        @pl.when((step >= 2) & (step < CHUNKS + 2))
        def _():
            c = step - 2
            b_wait(3, c)
            both = dq_send[1, :, chunk(c)].astype(jnp.float32) + dq_recv[3, :, chunk(c)].astype(jnp.float32)
            dq_send[1, :, chunk(c)] = both.astype(jnp.bfloat16)
            b_copy(1, c).start()

        @pl.when(step >= 3)
        def _():
            c = step - 3
            total = dq_acc[:, chunk(c)]
            for i in direct:
                b_wait(i, c)
                total = total + dq_recv[i, :, chunk(c)].astype(jnp.float32)
            finish(0, c, total)

    for i in range(n_rel):
        ld_copy(i).wait_send()

    @pl.loop(0, CHUNKS)
    def _(c):
        for array in range(4):
            for r in range(n_head - 1):
                in_copy(array, (q_ref, g_ref, k_ref, v_ref)[array], r, c).wait_send()
        for i in range(n_rel):
            for a in range(2):
                f_copy(i, c, a).wait_send()
            b_copy(i, c).wait_send()
        for array in range(3):
            for r in range(n_head - 1):
                o_copy(array, r, c).wait_send()
                o_copy(array, r, c).wait_recv()


def local(queries, keys, values, out_grad, log_sum_exp, row_delta, assignment, block_mask):
    n_head, n_blk = lax.axis_size("head"), lax.axis_size("blk")
    cycle = min(4, n_blk // 4)
    mults = [1, 2, -2, -1] + [m * f for m in range(3, cycle + 1) for f in (1, -1)]
    n_rel = len(mults)
    rows, width = queries.shape[1], queries.shape[2] // n_head
    total = rows * n_head
    heads = log_sum_exp.shape[0]
    pad = ((0, LANE_PAD - heads), (0, 0))
    ld = jnp.concatenate([
        jnp.pad(log_sum_exp[:, 0, :].astype(jnp.float32), pad),
        jnp.pad(row_delta[:, 0, :].astype(jnp.float32), pad),
    ])
    vmem = pl.BlockSpec(memory_space=pltpu.VMEM)
    smem = pl.BlockSpec(memory_space=pltpu.SMEM)
    dma = pltpu.SemaphoreType.DMA
    out = jax.ShapeDtypeStruct(queries.shape, jnp.bfloat16)
    bf, f32 = jnp.bfloat16, jnp.float32
    return pl.pallas_call(
        functools.partial(kernel, n_head, n_blk, mults),
        out_shape=(out, out, out),
        in_specs=[vmem] * 5 + [smem] * 2,
        out_specs=(vmem, vmem, vmem),
        scratch_shapes=[
            pltpu.VMEM((4, total, width), bf),
            pltpu.VMEM((n_rel, 2, total, width), bf),
            pltpu.VMEM((n_rel,) + ld.shape, f32),
            pltpu.VMEM((n_rel + 1, total, total), f32),
            pltpu.VMEM((total, width), f32),
            pltpu.VMEM((2, total, width), f32),
            pltpu.VMEM((3, total, width), bf),
            pltpu.VMEM((n_rel, total, width), bf),
            pltpu.VMEM((n_rel, total, width), bf),
            dma((4, n_head - 1, CHUNKS)), dma((4, n_head - 1, CHUNKS)),
            dma((n_rel,)), dma((n_rel,)),
            dma((n_rel, 2, CHUNKS)), dma((n_rel, 2, CHUNKS)),
            dma((n_rel, CHUNKS)), dma((n_rel, CHUNKS)),
            dma((3, n_head - 1, CHUNKS)), dma((3, n_head - 1, CHUNKS)),
        ],
        compiler_params=pltpu.CompilerParams(
            collective_id=0, has_side_effects=True, vmem_limit_bytes=48 * 1024 * 1024
        ),
    )(queries, keys, values, out_grad, ld, assignment, block_mask)


def solution(mesh):
    token = P("blk", "head", None)
    stat = P("head", "blk", None)
    return jax.shard_map(
        local,
        mesh=mesh,
        in_specs=(token, token, token, token, stat, stat, P(), P()),
        out_specs=(token, token, token),
        check_vma=False,
    )
```

```python
import functools

import jax
import jax.numpy as jnp
from jax import lax
from jax.experimental import pallas as pl
from jax.experimental.pallas import tpu as pltpu
from jax.sharding import PartitionSpec as P

HD = 128
LOG2E = 1.4426950408889634
BIG = 1e30
CHUNKS = 4
KV_PIECES = 2
FIRST = "i0 i1 i2 i3"
SECOND = "n0 n1 n2 n3 k0 k1"
THIRD = "f0 g0 f1 g1 f2 g2 f3 g3"
STEPS = ('h0', 'h1', 'h2', 'h3')
LANE_PAD = 16


def kernel(
    n_head,
    n_blk,
    mults,
    q_ref, k_ref, v_ref, g_ref, lse_hbm, delta_hbm, assign_hbm, mask_hbm,
    dq_out, dk_out, dv_out,
    qgkv, rqg, ld_ref, rld, bias, dq_acc, dkv_acc, fin, dq_send, dq_recv, stats, assign_ref, mask_ref,
    load, in_send, in_recv, kv_send, kv_recv, ld_send, ld_recv, f_send, f_recv, b_send, b_recv, o_send, o_recv,
):
    rows = q_ref.shape[1]
    width = q_ref.shape[2] // n_head
    total_rows = rows * n_head
    half = total_rows // 2
    heads = width // HD
    hc = heads // CHUNKS
    cw = hc * HD
    scaling = HD ** -0.5
    n_rel = len(mults)
    hi = lax.axis_index("head")
    me = lax.axis_index("blk")
    sign = 1 - 2 * lax.rem(me, 2)
    slots = [lax.rem(me + m * sign + 2 * n_blk, n_blk) for m in mults]
    landing = [i if m % 2 else mults.index(-m) for i, m in enumerate(mults)]
    sibling = hi + 1 - 2 * lax.rem(hi, 2)
    partners = [sibling, lax.rem(hi + 2, n_head), lax.rem(sibling + 2, n_head)]
    outs = (dq_out, dk_out, dv_out)
    ins = (q_ref, g_ref, k_ref, v_ref)
    my_rows = pl.ds(pl.multiple_of(hi * rows, rows), rows)
    my_cols = pl.ds(pl.multiple_of(hi * width, HD), width)
    near = hi // 2
    chip_rows = [pl.ds(pl.multiple_of(x * 2 * rows, 2 * rows), 2 * rows) for x in (near, 1 - near)]

    loads = [
        pltpu.make_async_copy(lse_hbm, stats.at[0], load.at[0]),
        pltpu.make_async_copy(delta_hbm, stats.at[1], load.at[1]),
        pltpu.make_async_copy(assign_hbm, assign_ref, load.at[2]),
        pltpu.make_async_copy(mask_hbm, mask_ref, load.at[3]),
    ] + [
        pltpu.make_async_copy(ref.at[0, :, my_cols], qgkv.at[array, my_rows, :], load.at[4 + array])
        for array, ref in enumerate(ins)
    ]
    for copy in loads:
        copy.start()

    barrier = pltpu.get_barrier_semaphore()
    for p in partners:
        pl.semaphore_signal(barrier, inc=1, device_id={"head": p}, device_id_type=pl.DeviceIdType.MESH)
    for s in slots:
        pl.semaphore_signal(barrier, inc=1, device_id={"blk": s}, device_id_type=pl.DeviceIdType.MESH)
    pl.semaphore_wait(barrier, n_head - 1 + n_rel)

    def remote(src, dst, send, recv, where):
        return pltpu.make_async_remote_copy(
            src_ref=src, dst_ref=dst, send_sem=send, recv_sem=recv,
            device_id=where, device_id_type=pl.DeviceIdType.MESH,
        )

    def chunk(c):
        return pl.ds(pl.multiple_of(c * cw, HD), cw)

    def in_copy(array, r, c):
        p = partners[r]
        return remote(
            ins[array].at[0, :, pl.ds(pl.multiple_of(p * width + c * cw, HD), cw)],
            qgkv.at[array, my_rows, chunk(c)],
            in_send.at[array, r, c], in_recv.at[array, r, c], {"head": p},
        )

    def kv_copy(array, r, piece):
        p = partners[r]
        kw = width // KV_PIECES
        return remote(
            ins[array].at[0, :, pl.ds(pl.multiple_of(p * width + piece * kw, HD), kw)],
            qgkv.at[array, my_rows, pl.ds(pl.multiple_of(piece * kw, HD), kw)],
            kv_send.at[array - 2, r, piece], kv_recv.at[array - 2, r, piece], {"head": p},
        )

    def ld_copy(i):
        return remote(ld_ref, rld.at[landing[i]], ld_send.at[i], ld_recv.at[landing[i]], {"blk": slots[i]})

    def ld_wait(i):
        remote(ld_ref, rld.at[i], ld_send.at[i], ld_recv.at[i], {"blk": slots[i]}).wait_recv()

    def f_copy(i, c, part):
        rs = chip_rows[part]
        if mults[i] == -1:
            return remote(rqg.at[1, :, rs, chunk(c)], rqg.at[3, :, rs, chunk(c)],
                          f_send.at[i, part, c], f_recv.at[i, part, c], {"blk": slots[0]})
        j = landing[i]
        return remote(qgkv.at[pl.ds(0, 2), rs, chunk(c)], rqg.at[j, :, rs, chunk(c)],
                      f_send.at[i, part, c], f_recv.at[j, part, c], {"blk": slots[i]})

    def f_wait(i, c, part):
        rs = chip_rows[part]
        remote(qgkv.at[pl.ds(0, 2), rs, chunk(c)], rqg.at[i, :, rs, chunk(c)],
               f_send.at[i, part, c], f_recv.at[i, part, c], {"blk": slots[i]}).wait_recv()

    def b_copy(i, c):
        if mults[i] == -1:
            j, where = 3, slots[0]
        else:
            j, where = landing[i], slots[i]
        return remote(dq_send.at[i, :, chunk(c)], dq_recv.at[j, :, chunk(c)],
                      b_send.at[i, c], b_recv.at[j, c], {"blk": where})

    def b_wait(i, c):
        remote(dq_send.at[i, :, chunk(c)], dq_recv.at[i, :, chunk(c)],
               b_send.at[i, c], b_recv.at[i, c], {"blk": slots[i]}).wait_recv()

    def o_copy(array, r, c):
        p = partners[r]
        return remote(
            fin.at[array, pl.ds(pl.multiple_of(p * rows, rows), rows), chunk(c)],
            outs[array].at[0, :, pl.ds(pl.multiple_of(hi * width + c * cw, HD), cw)],
            o_send.at[array, r, c], o_recv.at[array, r, c], {"head": p},
        )

    direct = [i for i, m in enumerate(mults) if m != -1]
    order = [2, 1] + [i for i in direct if i not in (1, 2)]

    def send_part(c, part):
        for r in ((0,), (1, 2))[part]:
            for array in range(2):
                in_copy(array, r, c).wait_recv()
        for i in order:
            f_copy(i, c, part).start()

    def forward(c, part):
        f_wait(1, c, part)
        f_copy(3, c, part).start()

    def start_in(c):
        for r in range(n_head - 1):
            for array in range(2):
                in_copy(array, r, c).start()

    def start_kv(piece):
        for r in range(n_head - 1):
            for array in (2, 3):
                kv_copy(array, r, piece).start()

    per = CHUNKS // KV_PIECES
    actions = {
        "i": start_in,
        "n": lambda c: send_part(c, 0),
        "f": lambda c: send_part(c, 1),
        "g": lambda c: forward(c, 0),
        "h": lambda c: forward(c, 1),
        "k": start_kv,
    }

    def act(plan):
        for word in plan.split():
            actions[word[0]](int(word[1:]))

    act(FIRST)
    for copy in loads[4:6]:
        copy.wait()
    act(SECOND)

    for copy in loads[:4]:
        copy.wait()
    for part in range(2):
        ld_ref[pl.ds(part * LANE_PAD, heads), :] = stats[part].astype(jnp.float32)
    for i in range(n_rel):
        ld_copy(i).start()

    key_ids = lax.broadcasted_iota(jnp.int32, (total_rows, total_rows), 0)
    query_ids = lax.broadcasted_iota(jnp.int32, (total_rows, total_rows), 1)
    key_low, query_low = key_ids < half, query_ids < half
    later = lax.rem(query_ids, half) >= lax.rem(key_ids, half)
    k_first = assign_ref[me]
    k_second = 2 * n_blk - 1 - k_first
    for i, s in enumerate([me] + slots):
        q_first = assign_ref[s]
        q_second = 2 * n_blk - 1 - q_first
        table = jnp.where(
            query_low,
            jnp.where(key_low, mask_ref[q_first, k_first], mask_ref[q_first, k_second]),
            jnp.where(key_low, mask_ref[q_second, k_first], mask_ref[q_second, k_second]),
        )
        allowed = (table == 1) | ((table == 2) & later)
        bias[i] = jnp.where(allowed, 0.0, -BIG)

    for copy in loads[6:]:
        copy.wait()
    act(THIRD)
    for i in range(n_rel):
        ld_wait(i)

    def pair(which, c, q_of, g_of, ld_of, first, emit):
        for h in range(hc):
            head = c * hc + h
            cols = pl.ds(pl.multiple_of(head * HD, HD), HD)
            q, g, k, v = q_of(cols), g_of(cols), qgkv[2, :, cols], qgkv[3, :, cols]
            lse = ld_of[pl.ds(head, 1), :] * LOG2E
            delta = ld_of[pl.ds(LANE_PAD + head, 1), :]
            contract = (((1,), (1,)), ((), ()))
            s = lax.dot_general(k, q, contract, preferred_element_type=jnp.float32)
            p = jnp.exp2(s * (scaling * LOG2E) - lse + bias[which])
            dp = lax.dot_general(v, g, contract, preferred_element_type=jnp.float32)
            ds = (p * (dp - delta)).astype(jnp.bfloat16)
            dv = jnp.dot(p.astype(jnp.bfloat16), g, preferred_element_type=jnp.float32)
            dk = jnp.dot(ds, q, preferred_element_type=jnp.float32)
            dq = lax.dot_general(ds, k, (((0,), (0,)), ((), ())), preferred_element_type=jnp.float32)
            if first:
                dkv_acc[0, :, cols] = dk
                dkv_acc[1, :, cols] = dv
            else:
                dkv_acc[0, :, cols] += dk
                dkv_acc[1, :, cols] += dv
            emit(cols, dq * scaling)

    def own(c):
        def emit(cols, dq):
            dq_acc[:, cols] = dq
        pair(0, c, lambda x: qgkv[0, :, x], lambda x: qgkv[1, :, x], ld_ref, True, emit)

    def other(i, c):
        def emit(cols, dq):
            dq_send[i, :, cols] = dq.astype(jnp.bfloat16)
        pair(i + 1, c, lambda x: rqg[i, 0, :, x], lambda x: rqg[i, 1, :, x], rld.at[i], False, emit)

    def finish(array, c, value):
        fin[array, :, chunk(c)] = value.astype(jnp.bfloat16)
        for r in range(n_head - 1):
            o_copy(array, r, c).start()
        outs[array][0, :, pl.ds(pl.multiple_of(hi * width + c * cw, HD), cw)] = fin[array, my_rows, chunk(c)]

    @pl.loop(0, CHUNKS + 3)
    def _(step):
        @pl.when(step < CHUNKS)
        def _():
            c = step
            for later_c in range(CHUNKS):
                @pl.when(c == later_c)
                def _():
                    act(STEPS[later_c])

            for piece in range(KV_PIECES):
                @pl.when(c == piece * per)
                def _():
                    for array in (2, 3):
                        for r in range(n_head - 1):
                            kv_copy(array, r, piece).wait_recv()
            own(c)
            for i in direct:
                if i != 1:
                    f_wait(i, c, 0)
                    f_wait(i, c, 1)
                    other(i, c)
                    b_copy(i, c).start()
            other(1, c)

        @pl.when((step >= 1) & (step < CHUNKS + 1))
        def _():
            c = step - 1
            f_wait(3, c, 0)
            f_wait(3, c, 1)
            other(3, c)
            b_copy(3, c).start()
            finish(1, c, dkv_acc[0, :, chunk(c)] * scaling)
            finish(2, c, dkv_acc[1, :, chunk(c)])

        @pl.when((step >= 2) & (step < CHUNKS + 2))
        def _():
            c = step - 2
            b_wait(3, c)
            both = dq_send[1, :, chunk(c)].astype(jnp.float32) + dq_recv[3, :, chunk(c)].astype(jnp.float32)
            dq_send[1, :, chunk(c)] = both.astype(jnp.bfloat16)
            b_copy(1, c).start()

        @pl.when(step >= 3)
        def _():
            c = step - 3
            total = dq_acc[:, chunk(c)]
            for i in direct:
                b_wait(i, c)
                total = total + dq_recv[i, :, chunk(c)].astype(jnp.float32)
            finish(0, c, total)

    for i in range(n_rel):
        ld_copy(i).wait_send()

    for piece in range(KV_PIECES):
        for r in range(n_head - 1):
            for array in (2, 3):
                kv_copy(array, r, piece).wait_send()

    @pl.loop(0, CHUNKS)
    def _(c):
        for array in range(2):
            for r in range(n_head - 1):
                in_copy(array, r, c).wait_send()
        for i in range(n_rel):
            for a in range(2):
                f_copy(i, c, a).wait_send()
            b_copy(i, c).wait_send()
        for array in range(3):
            for r in range(n_head - 1):
                o_copy(array, r, c).wait_send()
                o_copy(array, r, c).wait_recv()


def local(queries, keys, values, out_grad, log_sum_exp, row_delta, assignment, block_mask):
    n_head, n_blk = lax.axis_size("head"), lax.axis_size("blk")
    cycle = min(4, n_blk // 4)
    mults = [1, 2, -2, -1] + [m * f for m in range(3, cycle + 1) for f in (1, -1)]
    n_rel = len(mults)
    rows, width = queries.shape[1], queries.shape[2] // n_head
    total = rows * n_head
    vmem = pl.BlockSpec(memory_space=pltpu.VMEM)
    hbm = pl.BlockSpec(memory_space=pl.ANY)
    dma = pltpu.SemaphoreType.DMA
    out = jax.ShapeDtypeStruct(queries.shape, jnp.bfloat16)
    bf, f32 = jnp.bfloat16, jnp.float32
    return pl.pallas_call(
        functools.partial(kernel, n_head, n_blk, mults),
        out_shape=(out, out, out),
        in_specs=[hbm] * 8,
        out_specs=(vmem, vmem, vmem),
        scratch_shapes=[
            pltpu.VMEM((4, total, width), bf),
            pltpu.VMEM((n_rel, 2, total, width), bf),
            pltpu.VMEM((2 * LANE_PAD, total), f32),
            pltpu.VMEM((n_rel, 2 * LANE_PAD, total), f32),
            pltpu.VMEM((n_rel + 1, total, total), f32),
            pltpu.VMEM((total, width), f32),
            pltpu.VMEM((2, total, width), f32),
            pltpu.VMEM((3, total, width), bf),
            pltpu.VMEM((n_rel, total, width), bf),
            pltpu.VMEM((n_rel, total, width), bf),
            pltpu.VMEM((2, log_sum_exp.shape[0], total), bf),
            pltpu.SMEM(assignment.shape, jnp.int32),
            pltpu.SMEM(block_mask.shape, jnp.int32),
            dma((8,)),
            dma((2, n_head - 1, CHUNKS)), dma((2, n_head - 1, CHUNKS)),
            dma((2, n_head - 1, KV_PIECES)), dma((2, n_head - 1, KV_PIECES)),
            dma((n_rel,)), dma((n_rel,)),
            dma((n_rel, 2, CHUNKS)), dma((n_rel, 2, CHUNKS)),
            dma((n_rel, CHUNKS)), dma((n_rel, CHUNKS)),
            dma((3, n_head - 1, CHUNKS)), dma((3, n_head - 1, CHUNKS)),
        ],
        compiler_params=pltpu.CompilerParams(
            collective_id=0, has_side_effects=True, vmem_limit_bytes=60 * 1024 * 1024
        ),
    )(queries, keys, values, out_grad, log_sum_exp[:, 0], row_delta[:, 0], assignment, block_mask)


def solution(mesh):
    token = P("blk", "head", None)
    stat = P("head", "blk", None)
    return jax.shard_map(
        local,
        mesh=mesh,
        in_specs=(token, token, token, token, stat, stat, P(), P()),
        out_specs=(token, token, token),
        check_vma=False,
    )
```

```python
import functools

import jax
import jax.numpy as jnp
from jax import lax
from jax.experimental import pallas as pl
from jax.experimental.pallas import tpu as pltpu
from jax.sharding import PartitionSpec as P

HD = 128
LOG2E = 1.4426950408889634
BIG = 1e30
CHUNKS = 4
KV_PIECES = 2
FIRST = "i"
SECOND = "nk"
THIRD = ("f", "g")
STEP = "h"
LANE_PAD = 16


def kernel(
    n_head,
    n_blk,
    mults,
    q_ref, k_ref, v_ref, g_ref, lse_hbm, delta_hbm, assign_hbm, mask_hbm,
    dq_out, dk_out, dv_out,
    qgkv, rqg, ld_ref, rld, bias, dq_acc, dkv_acc, fin, dq_send, dq_recv, stats, assign_ref, mask_ref,
    load, in_send, in_recv, kv_send, kv_recv, ld_send, ld_recv, f_send, f_recv, b_send, b_recv, o_send, o_recv,
):
    rows = q_ref.shape[1]
    width = q_ref.shape[2] // n_head
    total_rows = rows * n_head
    half = total_rows // 2
    heads = width // HD
    hc = heads // CHUNKS
    cw = hc * HD
    scaling = HD ** -0.5
    n_rel = len(mults)
    hi = lax.axis_index("head")
    me = lax.axis_index("blk")
    sign = 1 - 2 * lax.rem(me, 2)
    slots = [lax.rem(me + m * sign + 2 * n_blk, n_blk) for m in mults]
    landing = [i if m % 2 else mults.index(-m) for i, m in enumerate(mults)]
    sibling = hi + 1 - 2 * lax.rem(hi, 2)
    partners = [sibling, lax.rem(hi + 2, n_head), lax.rem(sibling + 2, n_head)]
    outs = (dq_out, dk_out, dv_out)
    ins = (q_ref, g_ref, k_ref, v_ref)
    my_rows = pl.ds(pl.multiple_of(hi * rows, rows), rows)
    my_cols = pl.ds(pl.multiple_of(hi * width, HD), width)
    near = hi // 2
    chip_rows = [pl.ds(pl.multiple_of(x * 2 * rows, 2 * rows), 2 * rows) for x in (near, 1 - near)]

    loads = [
        pltpu.make_async_copy(lse_hbm, stats.at[0], load.at[0]),
        pltpu.make_async_copy(delta_hbm, stats.at[1], load.at[1]),
        pltpu.make_async_copy(assign_hbm, assign_ref, load.at[2]),
        pltpu.make_async_copy(mask_hbm, mask_ref, load.at[3]),
    ] + [
        pltpu.make_async_copy(ref.at[0, :, my_cols], qgkv.at[array, my_rows, :], load.at[4 + array])
        for array, ref in enumerate(ins)
    ]
    for copy in loads:
        copy.start()

    barrier = pltpu.get_barrier_semaphore()
    for p in partners:
        pl.semaphore_signal(barrier, inc=1, device_id={"head": p}, device_id_type=pl.DeviceIdType.MESH)
    for s in slots:
        pl.semaphore_signal(barrier, inc=1, device_id={"blk": s}, device_id_type=pl.DeviceIdType.MESH)
    pl.semaphore_wait(barrier, n_head - 1 + n_rel)

    def remote(src, dst, send, recv, where):
        return pltpu.make_async_remote_copy(
            src_ref=src, dst_ref=dst, send_sem=send, recv_sem=recv,
            device_id=where, device_id_type=pl.DeviceIdType.MESH,
        )

    def chunk(c):
        return pl.ds(pl.multiple_of(c * cw, HD), cw)

    def in_copy(array, r, c):
        p = partners[r]
        return remote(
            ins[array].at[0, :, pl.ds(pl.multiple_of(p * width + c * cw, HD), cw)],
            qgkv.at[array, my_rows, chunk(c)],
            in_send.at[array, r, c], in_recv.at[array, r, c], {"head": p},
        )

    def kv_copy(array, r, piece):
        p = partners[r]
        kw = width // KV_PIECES
        return remote(
            ins[array].at[0, :, pl.ds(pl.multiple_of(p * width + piece * kw, HD), kw)],
            qgkv.at[array, my_rows, pl.ds(pl.multiple_of(piece * kw, HD), kw)],
            kv_send.at[array - 2, r, piece], kv_recv.at[array - 2, r, piece], {"head": p},
        )

    def ld_copy(i):
        return remote(ld_ref, rld.at[landing[i]], ld_send.at[i], ld_recv.at[landing[i]], {"blk": slots[i]})

    def ld_wait(i):
        remote(ld_ref, rld.at[i], ld_send.at[i], ld_recv.at[i], {"blk": slots[i]}).wait_recv()

    def f_copy(i, c, part):
        rs = chip_rows[part]
        if mults[i] == -1:
            return remote(rqg.at[1, :, rs, chunk(c)], rqg.at[3, :, rs, chunk(c)],
                          f_send.at[i, part, c], f_recv.at[i, part, c], {"blk": slots[0]})
        j = landing[i]
        return remote(qgkv.at[pl.ds(0, 2), rs, chunk(c)], rqg.at[j, :, rs, chunk(c)],
                      f_send.at[i, part, c], f_recv.at[j, part, c], {"blk": slots[i]})

    def f_wait(i, c, part):
        rs = chip_rows[part]
        remote(qgkv.at[pl.ds(0, 2), rs, chunk(c)], rqg.at[i, :, rs, chunk(c)],
               f_send.at[i, part, c], f_recv.at[i, part, c], {"blk": slots[i]}).wait_recv()

    def b_copy(i, c):
        if mults[i] == -1:
            j, where = 3, slots[0]
        else:
            j, where = landing[i], slots[i]
        return remote(dq_send.at[i, :, chunk(c)], dq_recv.at[j, :, chunk(c)],
                      b_send.at[i, c], b_recv.at[j, c], {"blk": where})

    def b_wait(i, c):
        remote(dq_send.at[i, :, chunk(c)], dq_recv.at[i, :, chunk(c)],
               b_send.at[i, c], b_recv.at[i, c], {"blk": slots[i]}).wait_recv()

    def o_copy(array, r, c):
        p = partners[r]
        return remote(
            fin.at[array, pl.ds(pl.multiple_of(p * rows, rows), rows), chunk(c)],
            outs[array].at[0, :, pl.ds(pl.multiple_of(hi * width + c * cw, HD), cw)],
            o_send.at[array, r, c], o_recv.at[array, r, c], {"head": p},
        )

    direct = [i for i, m in enumerate(mults) if m != -1]
    order = [2, 1] + [i for i in direct if i not in (1, 2)]

    def send_part(c, part):
        for r in ((0,), (1, 2))[part]:
            for array in range(2):
                in_copy(array, r, c).wait_recv()
        for i in order:
            f_copy(i, c, part).start()

    def forward(c, part):
        f_wait(1, c, part)
        f_copy(3, c, part).start()

    def start_in(c):
        for r in range(n_head - 1):
            for array in range(2):
                in_copy(array, r, c).start()

    def start_kv(piece):
        for r in range(n_head - 1):
            for array in (2, 3):
                kv_copy(array, r, piece).start()

    per = CHUNKS // KV_PIECES
    actions = {
        "i": start_in,
        "n": lambda c: send_part(c, 0),
        "f": lambda c: send_part(c, 1),
        "g": lambda c: forward(c, 0),
        "h": lambda c: forward(c, 1),
        "k": start_kv,
    }

    def act(plan):
        for name in plan:
            for c in range(KV_PIECES if name == "k" else CHUNKS):
                actions[name](c)

    act(FIRST)
    for copy in loads[4:6]:
        copy.wait()
    act(SECOND)

    for copy in loads[:4]:
        copy.wait()
    for part in range(2):
        ld_ref[pl.ds(part * LANE_PAD, heads), :] = stats[part].astype(jnp.float32)
    for i in range(n_rel):
        ld_copy(i).start()

    key_ids = lax.broadcasted_iota(jnp.int32, (total_rows, total_rows), 0)
    query_ids = lax.broadcasted_iota(jnp.int32, (total_rows, total_rows), 1)
    key_low, query_low = key_ids < half, query_ids < half
    later = lax.rem(query_ids, half) >= lax.rem(key_ids, half)
    k_first = assign_ref[me]
    k_second = 2 * n_blk - 1 - k_first
    for i, s in enumerate([me] + slots):
        q_first = assign_ref[s]
        q_second = 2 * n_blk - 1 - q_first
        table = jnp.where(
            query_low,
            jnp.where(key_low, mask_ref[q_first, k_first], mask_ref[q_first, k_second]),
            jnp.where(key_low, mask_ref[q_second, k_first], mask_ref[q_second, k_second]),
        )
        allowed = (table == 1) | ((table == 2) & later)
        bias[i] = jnp.where(allowed, 0.0, -BIG)

    for copy in loads[6:]:
        copy.wait()
    for group in THIRD:
        for c in range(CHUNKS):
            for name in group:
                actions[name](c)
    for i in range(n_rel):
        ld_wait(i)

    def pair(which, c, q_of, g_of, ld_of, first, emit):
        for h in range(hc):
            head = c * hc + h
            cols = pl.ds(pl.multiple_of(head * HD, HD), HD)
            q, g, k, v = q_of(cols), g_of(cols), qgkv[2, :, cols], qgkv[3, :, cols]
            lse = ld_of[pl.ds(head, 1), :] * LOG2E
            delta = ld_of[pl.ds(LANE_PAD + head, 1), :]
            contract = (((1,), (1,)), ((), ()))
            s = lax.dot_general(k, q, contract, preferred_element_type=jnp.float32)
            p = jnp.exp2(s * (scaling * LOG2E) - lse + bias[which])
            dp = lax.dot_general(v, g, contract, preferred_element_type=jnp.float32)
            ds = (p * (dp - delta)).astype(jnp.bfloat16)
            dv = jnp.dot(p.astype(jnp.bfloat16), g, preferred_element_type=jnp.float32)
            dk = jnp.dot(ds, q, preferred_element_type=jnp.float32)
            dq = lax.dot_general(ds, k, (((0,), (0,)), ((), ())), preferred_element_type=jnp.float32)
            if first:
                dkv_acc[0, :, cols] = dk
                dkv_acc[1, :, cols] = dv
            else:
                dkv_acc[0, :, cols] += dk
                dkv_acc[1, :, cols] += dv
            emit(cols, dq * scaling)

    def own(c):
        def emit(cols, dq):
            dq_acc[:, cols] = dq
        pair(0, c, lambda x: qgkv[0, :, x], lambda x: qgkv[1, :, x], ld_ref, True, emit)

    def other(i, c):
        def emit(cols, dq):
            dq_send[i, :, cols] = dq.astype(jnp.bfloat16)
        pair(i + 1, c, lambda x: rqg[i, 0, :, x], lambda x: rqg[i, 1, :, x], rld.at[i], False, emit)

    def finish(array, c, value):
        fin[array, :, chunk(c)] = value.astype(jnp.bfloat16)
        for r in range(n_head - 1):
            o_copy(array, r, c).start()
        outs[array][0, :, pl.ds(pl.multiple_of(hi * width + c * cw, HD), cw)] = fin[array, my_rows, chunk(c)]

    @pl.loop(0, CHUNKS + 3)
    def _(step):
        @pl.when(step < CHUNKS)
        def _():
            c = step
            for name in STEP:
                actions[name](c)

            for piece in range(KV_PIECES):
                @pl.when(c == piece * per)
                def _():
                    for array in (2, 3):
                        for r in range(n_head - 1):
                            kv_copy(array, r, piece).wait_recv()
            own(c)
            for i in direct:
                if i != 1:
                    f_wait(i, c, 0)
                    f_wait(i, c, 1)
                    other(i, c)
                    b_copy(i, c).start()
            other(1, c)

        @pl.when((step >= 1) & (step < CHUNKS + 1))
        def _():
            c = step - 1
            f_wait(3, c, 0)
            f_wait(3, c, 1)
            other(3, c)
            b_copy(3, c).start()
            finish(1, c, dkv_acc[0, :, chunk(c)] * scaling)
            finish(2, c, dkv_acc[1, :, chunk(c)])

        @pl.when((step >= 2) & (step < CHUNKS + 2))
        def _():
            c = step - 2
            b_wait(3, c)
            both = dq_send[1, :, chunk(c)].astype(jnp.float32) + dq_recv[3, :, chunk(c)].astype(jnp.float32)
            dq_send[1, :, chunk(c)] = both.astype(jnp.bfloat16)
            b_copy(1, c).start()

        @pl.when(step >= 3)
        def _():
            c = step - 3
            total = dq_acc[:, chunk(c)]
            for i in direct:
                b_wait(i, c)
                total = total + dq_recv[i, :, chunk(c)].astype(jnp.float32)
            finish(0, c, total)

    for i in range(n_rel):
        ld_copy(i).wait_send()

    for piece in range(KV_PIECES):
        for r in range(n_head - 1):
            for array in (2, 3):
                kv_copy(array, r, piece).wait_send()

    @pl.loop(0, CHUNKS)
    def _(c):
        for array in range(2):
            for r in range(n_head - 1):
                in_copy(array, r, c).wait_send()
        for i in range(n_rel):
            for a in range(2):
                f_copy(i, c, a).wait_send()
            b_copy(i, c).wait_send()
        for array in range(3):
            for r in range(n_head - 1):
                o_copy(array, r, c).wait_send()
                o_copy(array, r, c).wait_recv()


def local(queries, keys, values, out_grad, log_sum_exp, row_delta, assignment, block_mask):
    n_head, n_blk = lax.axis_size("head"), lax.axis_size("blk")
    cycle = min(4, n_blk // 4)
    mults = [1, 2, -2, -1] + [m * f for m in range(3, cycle + 1) for f in (1, -1)]
    n_rel = len(mults)
    rows, width = queries.shape[1], queries.shape[2] // n_head
    total = rows * n_head
    vmem = pl.BlockSpec(memory_space=pltpu.VMEM)
    hbm = pl.BlockSpec(memory_space=pl.ANY)
    dma = pltpu.SemaphoreType.DMA
    out = jax.ShapeDtypeStruct(queries.shape, jnp.bfloat16)
    bf, f32 = jnp.bfloat16, jnp.float32
    return pl.pallas_call(
        functools.partial(kernel, n_head, n_blk, mults),
        out_shape=(out, out, out),
        in_specs=[hbm] * 8,
        out_specs=(vmem, vmem, vmem),
        scratch_shapes=[
            pltpu.VMEM((4, total, width), bf),
            pltpu.VMEM((n_rel, 2, total, width), bf),
            pltpu.VMEM((2 * LANE_PAD, total), f32),
            pltpu.VMEM((n_rel, 2 * LANE_PAD, total), f32),
            pltpu.VMEM((n_rel + 1, total, total), f32),
            pltpu.VMEM((total, width), f32),
            pltpu.VMEM((2, total, width), f32),
            pltpu.VMEM((3, total, width), bf),
            pltpu.VMEM((n_rel, total, width), bf),
            pltpu.VMEM((n_rel, total, width), bf),
            pltpu.VMEM((2, log_sum_exp.shape[0], total), bf),
            pltpu.SMEM(assignment.shape, jnp.int32),
            pltpu.SMEM(block_mask.shape, jnp.int32),
            dma((8,)),
            dma((2, n_head - 1, CHUNKS)), dma((2, n_head - 1, CHUNKS)),
            dma((2, n_head - 1, KV_PIECES)), dma((2, n_head - 1, KV_PIECES)),
            dma((n_rel,)), dma((n_rel,)),
            dma((n_rel, 2, CHUNKS)), dma((n_rel, 2, CHUNKS)),
            dma((n_rel, CHUNKS)), dma((n_rel, CHUNKS)),
            dma((3, n_head - 1, CHUNKS)), dma((3, n_head - 1, CHUNKS)),
        ],
        compiler_params=pltpu.CompilerParams(
            collective_id=0, has_side_effects=True, vmem_limit_bytes=60 * 1024 * 1024
        ),
    )(queries, keys, values, out_grad, log_sum_exp[:, 0], row_delta[:, 0], assignment, block_mask)


def solution(mesh):
    token = P("blk", "head", None)
    stat = P("head", "blk", None)
    return jax.shard_map(
        local,
        mesh=mesh,
        in_specs=(token, token, token, token, stat, stat, P(), P()),
        out_specs=(token, token, token),
        check_vma=False,
    )
```
